256 devices in a mesh: fsdp: 32 (over y, z), tp: 8 (over x, core).
Axes of the slice: x: 4, y: 4, z: 8, core: 2. Of those that a mesh axis runs over, the one named last changes fastest.
Arguments:
- hidden: bfloat16 [4096, 14336], P('fsdp', 'tp'), may hold values from -6 to 6
- residual: bfloat16 [4096, 8192], P('tp', 'fsdp'), may hold values from -22 to 22
- target: bfloat16 [4096, 8192], P('tp', 'fsdp'), may hold values from -8.2 to 8.2
- norm_gain: float32 [8192], P('fsdp'), may hold values from 0.1 to 1.9
- weight: bfloat16 [14336, 8192], P('tp', 'fsdp'), may hold values from -0.03775065 to 0.03775065
- v_prev: float32 [14336, 8192], P('tp', 'fsdp'), may hold values from -6 to 6
- v_cur: float32 [14336, 8192], P('tp', 'fsdp'), may hold values from -6.3 to 6.3
- beta_prev: float32 [], replicated, may hold values from 0.125 to 0.375
Outputs:
- v_next: float32 [14336, 8192], P('tp', 'fsdp')
- alpha: float32 [], replicated
- beta: float32 [], replicated
The draws below stay inside these ranges and needn't reach their ends.
All inputs are finite; a program needn't handle non-finite values.
Results may differ from the reference program's by a relative error of at most 0.0047.
Values may be sent and summed in bfloat16 or wider, within the bound.
A program may use at most 128 MiB of HBM per device.

```python
import math
import jax
import jax.numpy as jnp
from jax import lax

D = 8192
FF = 14336
TOKENS = 4096


ROOT_TWO = math.sqrt(2.0)


TAIL_LEVEL = 3.4e-06


def column_rise(width):
    position = jnp.arange(width, dtype=jnp.float32) / (width - 1)
    return 0.6 * jnp.exp(position * math.log(3.0))


def shared_levels(key, marker, rows, cols):
    levels = jax.random.uniform(jax.random.fold_in(key, marker), (rows, cols), jnp.float32)
    return jnp.clip(levels, TAIL_LEVEL, 1.0 - TAIL_LEVEL)


def normal_from(levels):
    return ROOT_TWO * lax.erf_inv(2.0 * levels - 1.0)


def draw_residual(key, part):
    levels = shared_levels(key, 101, TOKENS, D)
    field = normal_from(levels)
    return (field * column_rise(D)[None, :]).astype(jnp.bfloat16)


def draw_target(key, part):
    levels = shared_levels(key, 101, TOKENS, D)
    key = jax.random.fold_in(key, 5)
    lean_key, noise_key = jax.random.split(key)
    lean = jax.random.uniform(lean_key, (TOKENS, 1), jnp.float32, -1.0, 1.5)
    shared = normal_from(levels)
    noise = jax.random.truncated_normal(noise_key, -4.5, 4.5, (TOKENS, D), jnp.float32)
    return (0.8 * lean * shared + 0.6 * noise).astype(jnp.bfloat16)


def draw_weight(key, part):
    levels = shared_levels(key, 202, FF, D)
    shared = normal_from(levels)
    return (shared * (1.0 / math.sqrt(FF))).astype(jnp.bfloat16)


def draw_v_cur(key, part):
    levels = shared_levels(key, 202, FF, D)
    key = jax.random.fold_in(key, 9)
    shared = normal_from(levels)
    noise = jax.random.truncated_normal(key, -4.5, 4.5, (FF, D), jnp.float32)
    return 0.8 * shared + 0.6 * noise


def level_of(rng, dims, cuts, low, largest):
    gain, own = 1.0, jax.random.fold_in(rng, 6)
    for dim, shards_of in cuts:
        draws = jnp.exp(jax.random.uniform(jax.random.fold_in(own, dim), (shards_of,), jnp.float32, low / len(cuts), largest / len(cuts)))
        gain = gain * jnp.repeat(draws, dims[dim] // shards_of).reshape([-1 if axis == dim else 1 for axis in range(len(dims))])
    return gain


def centred(key, shape, spread, most, cuts=(), kind=jnp.bfloat16):
    drawn = spread * jax.random.normal(key, shape, jnp.float32)
    if cuts:
        drawn = drawn * level_of(key, shape, cuts, -0.22, 0.18)
    return jnp.clip(drawn, -most, most).astype(kind)


def setup_inputs(seed: int = 0) -> dict:
    streams_of = jax.random.split(jax.random.key(seed), 9)
    hidden = centred(streams_of[0], (TOKENS, FF), 1.0, 6.0, ((0, 32), (1, 8)))
    residual = draw_residual(jax.random.fold_in(streams_of[8], 71), 0)
    target = draw_target(jax.random.fold_in(streams_of[8], 71), 0)
    norm_gain = jnp.clip(1.0 + 0.18 * jax.random.normal(streams_of[3], (D,), jnp.float32), 0.1, 1.9)
    weight = draw_weight(jax.random.fold_in(streams_of[8], 71), 0)
    v_prev = centred(streams_of[5], (FF, D), 1.0, 6.0, ((0, 8), (1, 32)), jnp.float32)
    v_cur = draw_v_cur(jax.random.fold_in(streams_of[8], 71), 0)
    beta_prev = jnp.clip(jax.random.uniform(streams_of[7], (), jnp.float32, 0.125, 0.375), 0.125, 0.375)
    return dict(hidden=hidden, residual=residual, target=target, norm_gain=norm_gain, weight=weight, v_prev=v_prev, v_cur=v_cur, beta_prev=beta_prev)


EPSILON = 1e-05

def reference(hidden, residual, target, norm_gain, weight, v_prev, v_cur, beta_prev):
    tangent_bf = v_cur.astype(jnp.bfloat16)
    outputs = residual.astype(jnp.float32) + jnp.dot(hidden, weight, preferred_element_type=jnp.float32)
    tangent = jnp.dot(hidden, tangent_bf, preferred_element_type=jnp.float32)
    target_f = target.astype(jnp.float32)
    radius = jnp.sqrt(lax.optimization_barrier(jnp.sum(outputs * outputs, axis=1, keepdims=True)) / D + EPSILON)
    normed = outputs / radius
    adjoint = norm_gain * (norm_gain * normed - target_f)
    centre = lax.optimization_barrier(jnp.sum(normed * adjoint, axis=1, keepdims=True)) / D
    stretch = lax.optimization_barrier(jnp.sum(normed * tangent, axis=1, keepdims=True)) / D
    normed_dot = (tangent - normed * stretch) / radius
    adjoint_dot = norm_gain * norm_gain * normed_dot
    centre_dot = lax.optimization_barrier(jnp.sum(normed_dot * adjoint + normed * adjoint_dot, axis=1, keepdims=True)) / D
    hessian_rows = (adjoint_dot - normed_dot * centre - normed * centre_dot - (adjoint - normed * centre) * (stretch / radius)) / (TOKENS * radius)
    hessian_rows = hessian_rows.astype(jnp.bfloat16)
    product = lax.dot_general(hidden, hessian_rows, (((0,), (0,)), ((), ())), preferred_element_type=jnp.float32)
    scale = 1.0 / (FF * D)
    update = product - beta_prev * v_prev
    alpha = jnp.sum(update * v_cur) * scale
    update = update - alpha * v_cur
    beta = jnp.sqrt(jnp.sum(update * update) * scale)
    return (update / beta, alpha, beta)
```

```python
import jax
import jax.numpy as jnp
from jax import lax
from jax.sharding import PartitionSpec as P

D = 8192
FF = 14336


EPSILON = 1e-05


def on_device(hidden, residual, target, norm_gain, weight, v_prev, v_cur, beta_prev):
    columns = weight.shape[1]
    stacked = jnp.concatenate([weight, v_cur.astype(jnp.bfloat16)], axis=1)
    gathered = lax.all_gather(hidden, "fsdp", axis=0, tiled=True)
    total_rows = gathered.shape[0]
    sums = lax.psum_scatter(
        jnp.dot(gathered, stacked, preferred_element_type=jnp.float32),
        "tp",
        scatter_dimension=0,
        tiled=True,
    )
    o = residual.astype(jnp.float32) + sums[:, :columns]
    t = sums[:, columns:]
    y = target.astype(jnp.float32) * norm_gain
    g2 = norm_gain * norm_gain
    parts = jnp.stack(
        [
            jnp.sum(o * o, axis=1),
            jnp.sum(g2 * o * o, axis=1),
            jnp.sum(y * o, axis=1),
            jnp.sum(o * t, axis=1),
            jnp.sum(g2 * o * t, axis=1),
            jnp.sum(y * t, axis=1),
        ]
    )
    s_oo, s_goo, s_yo, s_ot, s_got, s_yt = lax.psum(parts, "fsdp")[:, :, None]
    inv = 1.0 / jnp.sqrt(s_oo / D + EPSILON)
    stretch = s_ot * inv / D
    centre = (s_goo * inv - s_yo) * inv / D
    tilt = stretch * inv
    centre_dot = (2.0 * inv * s_got - s_yt + tilt * (s_yo - 2.0 * inv * s_goo)) * inv / D
    normed = o * inv
    normed_dot = (t - normed * stretch) * inv
    rows = (
        (g2 - centre) * (normed_dot - normed * tilt) - normed * centre_dot + y * tilt
    ) * (inv / total_rows)
    rows = rows.astype(jnp.bfloat16)
    product = lax.dot_general(
        gathered,
        lax.all_gather(rows, "tp", axis=0, tiled=True),
        (((0,), (0,)), ((), ())),
        preferred_element_type=jnp.float32,
    )
    scale = 1.0 / (FF * D)
    update = product - beta_prev * v_prev
    v_sq = jnp.sum(v_cur * v_cur)
    along = jnp.sum(update * v_cur)
    own = along / jnp.maximum(v_sq, 1e-30)
    left = update - own * v_cur
    facts = jnp.stack([v_sq, along, own, jnp.sum(left * left), jnp.sum(left * v_cur)])
    facts = lax.all_gather(facts, ("fsdp", "tp"))
    alpha = jnp.sum(facts[:, 1]) * scale
    shift = facts[:, 2] - alpha
    beta = jnp.sqrt(
        jnp.sum(facts[:, 3] + shift * (shift * facts[:, 0] + 2.0 * facts[:, 4])) * scale
    )
    return ((update - alpha * v_cur) / beta, alpha, beta)


def solution(mesh):
    return jax.shard_map(
        on_device,
        mesh=mesh,
        in_specs=(
            P("fsdp", "tp"),
            P("tp", "fsdp"),
            P("tp", "fsdp"),
            P("fsdp"),
            P("tp", "fsdp"),
            P("tp", "fsdp"),
            P("tp", "fsdp"),
            P(),
        ),
        out_specs=(P("tp", "fsdp"), P(), P()),
        check_vma=False,
    )
```

```python
import functools

import jax
import jax.numpy as jnp
from jax import lax
from jax.experimental import pallas as pl
from jax.experimental.pallas import tpu as pltpu
from jax.sharding import PartitionSpec as P

D = 8192
FF = 14336
EPSILON = 1e-05

NY, NZ, NT = 4, 8, 8
STAGES = 4
SPLIT = 1024
LEAD = 1
SCHEDULE = [
    (0, -1), (1, 0), ("pair", 6), (2, 1), ("stats", 6), (3, 2), ("stats_y", 6), (4, 3),
    ("hessian", 6), (5, 4), ("share", 6), (6, 5), ("forward", 5), ("backward", 6),
]
BF, F32 = jnp.bfloat16, jnp.float32
MESH = pl.DeviceIdType.MESH


def gather_plan(ff):
    cols = {"a": (0, SPLIT), "b": (SPLIT, ff - SPLIT)}
    size = {"y": NY, "z": NZ}
    order = {"a": ("z", "y"), "b": ("y", "z")}
    slots = {}

    def slot(key):
        return slots.setdefault(key, len(slots))

    def arrivals(part, first, second):
        axes = order[part]
        start, width = cols[part]
        offs = (first, second)
        level = 1 if second else 0
        off, n = offs[level], size[axes[level]]
        if abs(off) * 2 == n:
            half = width // 2
            return [
                ((part, first, second, 0), (start, half), axes[level], -1),
                ((part, first, second, 1), (start + half, half), axes[level], 1),
            ]
        step = -1 if off > 0 else 1
        return [((part, first, second, 0), (start, width), axes[level], step)]

    def offsets(n):
        return [0] + [s * d for d in range(1, n // 2) for s in (1, -1)] + [n // 2]

    waves = [[] for _ in range(NY // 2 + NZ // 2 + 1)]
    for part in ("b", "a"):
        n1, n2 = (size[axis] for axis in order[part])
        for first in offsets(n1):
            for second in offsets(n2):
                recvs = []
                if first or second:
                    recvs = [(slot(key), c) for key, c, _, _ in arrivals(part, first, second)]
                sends = []

                def forward(nf, ns, step):
                    for key, c, axis, s in arrivals(part, nf, ns):
                        if s == step:
                            sends.append((slot(key), c, axis, step))

                for off, n, grow in (
                    (second, n2, lambda o: (first, o)),
                    (first, n1, lambda o: (o, 0)),
                ):
                    if grow(0)[1] == 0 and grow(1)[1] == 0 and second:
                        continue
                    if off >= 0 and off < n // 2:
                        forward(*grow(off + 1), -1)
                    if off <= 0 and -off < n // 2:
                        o = off - 1
                        forward(*grow(n // 2 if -o == n // 2 else o), 1)
                where = (first, second) if order[part][0] == "y" else (second, first)
                waves[abs(first) + abs(second)].append((where, recvs, sends))
    return waves, len(slots)

def kernel(
    hidden, residual, target, gain, weight, v_prev, v_cur, beta_prev,
    update, facts_out,
    hid, w, vb, vc, vp, res, tar, sib_out, sib_in, half, x_out, x_in, o_s, t_s, stat_z, stat_y,
    rows_s, prod, fact_z, fact_y, fact_t,
    local_sem, hid_recv, sib_recv, x_recv, z_recv, y_recv, rows_recv, fact_recv,
    send_sem, fact_send,
):
    stages, n_blocks, rows, ff = hid.shape
    four = 4 * rows
    cols = w.shape[1]
    tokens = stages * n_blocks * rows
    fs, tp = lax.axis_index("fsdp"), lax.axis_index("tp")
    y, z = fs // NZ, fs % NZ
    x, core = tp // 2, tp % 2
    waves, _ = gather_plan(ff)
    ys = [(y + d) % NY for d in range(NY)]
    zs = [(z + d) % NZ for d in range(NZ)]
    z_place = [(q // 4) * 16 + q % 4 for q in zs]

    def place(dy, dz):
        return z_place[dz % NZ] + ys[dy % NY] * 4

    me = place(0, 0)

    def at(dy=0, dz=0):
        return (ys[dy % NY] * NZ + zs[dz % NZ], tp)

    def at_x(dx):
        return (fs, ((x + dx) % 4) * 2 + core)

    sibling = (fs, x * 2 + 1 - core)

    loads = [
        pltpu.make_async_copy(hidden.at[pl.ds(k * rows, rows)], hid.at[k, me], local_sem.at[k])
        for k in range(stages)
    ]
    for n, (src, dst) in enumerate(
        ((weight, w), (v_cur, vc), (residual, res), (target, tar), (v_prev, vp))
    ):
        loads.append(pltpu.make_async_copy(src, dst, local_sem.at[stages + n]))
    for load in loads:
        load.start()

    barrier = pltpu.get_barrier_semaphore()
    peers = [at(dy=d) for d in range(1, NY)] + [at(dz=d) for d in range(1, NZ)]
    peers += [(fs, (tp + d) % NT) for d in range(1, NT)]
    for peer in peers:
        pl.semaphore_signal(barrier, inc=1, device_id=peer, device_id_type=MESH)
    pl.semaphore_wait(barrier, len(peers))

    def remote(src, dst, send, recv, to):
        return pltpu.make_async_remote_copy(
            src_ref=src, dst_ref=dst, send_sem=send, recv_sem=recv,
            device_id=to, device_id_type=MESH,
        )

    def hid_copy(k, block, slot, columns, to):
        ref = hid.at[k, block, :, pl.ds(*columns)]
        return remote(ref, ref, send_sem.at[0, k], hid_recv.at[k, slot], to)

    def wave(d, k):
        for where, recvs, sends in waves[d]:
            block = place(*where)
            for slot, columns in recvs:
                hid_copy(k, block, slot, columns, sibling).wait_recv()
            for slot, columns, axis, step in sends:
                to = at(dy=step) if axis == "y" else at(dz=step)
                hid_copy(k, block, slot, columns, to).start()

    def dot_rows(k, c, write):
        def tile(i, carry):
            lhs = hid[k, pl.ds(c * 16 + i * 8, 8)].reshape(8 * rows, ff)
            for n, rhs in enumerate((w, vb)):
                out = jnp.dot(lhs, rhs[...], preferred_element_type=F32)
                write(i, n, out.reshape(2, four, cols))
            return carry

        lax.fori_loop(0, 2, tile, 0)

    def sib_copy(k):
        return remote(sib_out.at[k], sib_in.at[k], send_sem.at[1, k], sib_recv.at[k], sibling)

    def forward(k):
        def to_sibling(i, n, out):
            sib_out[k, pl.ds(i * 2, 2), :, pl.ds(n * cols, cols)] = out.astype(BF)

        def to_half(i, n, out):
            half[pl.ds(i * 2, 2), :, pl.ds(n * cols, cols)] = out

        dot_rows(k, 1 - core, to_sibling)
        sib_copy(k).start()
        dot_rows(k, core, to_half)

    def x_copy(k, dx, slot):
        there = (x + dx) % 4
        return remote(
            x_out.at[k, there], x_in.at[k, slot], send_sem.at[2, k], x_recv.at[k, slot], at_x(dx)
        )

    def pair(k):
        sib_copy(k).wait_recv()
        for dx in (2, 1, 3):
            there = (x + dx) % 4
            x_out[k, there] = (half[there] + sib_in[k, there].astype(F32)).astype(BF)
            x_copy(k, dx, x).start()
        half[x] = half[x] + sib_in[k, x].astype(F32)

    def token_rows(ref, k):
        return jnp.concatenate(
            [ref[pl.ds(j * stages * rows + k * rows, rows), :].astype(F32) for j in range(4)], axis=0
        )

    def z_copy(k, dz):
        src = stat_z.at[k, z]
        return remote(src, src, send_sem.at[3, k], z_recv.at[k, z], at(dz=dz))

    def y_copy(k, dy):
        src = stat_y.at[k, y]
        return remote(src, src, send_sem.at[4, k], y_recv.at[k, y], at(dy=dy))

    lane = lax.broadcasted_iota(jnp.int32, (four, 128), 1)

    def stats(k):
        total = half[x]
        for dx in (1, 3, 2):
            there = (x + dx) % 4
            x_copy(k, dx, there).wait_recv()
            total = total + x_in[k, there].astype(F32)
        o = total[:, :cols] + token_rows(res, k)
        t = total[:, cols:]
        g = gain[...]
        gy = token_rows(tar, k) * g
        o_s[k] = o
        t_s[k] = t
        g2o = g * g * o
        packed = jnp.zeros((four, 128), F32)
        for n, term in enumerate((o * o, g2o * o, gy * o, o * t, g2o * t, gy * t)):
            packed = jnp.where(lane == n, jnp.sum(term, axis=1, keepdims=True), packed)
        stat_z[k, z] = packed.T[:8]
        for dz in (4, 3, 5, 2, 6, 1, 7):
            z_copy(k, dz).start()

    def stats_y(k):
        for dz in range(1, NZ):
            there = zs[dz]
            ref = stat_z.at[k, there]
            remote(ref, ref, send_sem.at[3, k], z_recv.at[k, there], sibling).wait_recv()
        stat_y[k, y] = jnp.sum(stat_z[k], axis=0)
        for dy in (2, 1, 3):
            y_copy(k, dy).start()

    def rows_copy(k, cc, xx, sem, to):
        ref = rows_s.at[k, cc * 4 + xx]
        return remote(ref, ref, send_sem.at[5, k], rows_recv.at[k, sem], to)

    def hessian(k):
        for dy in range(1, NY):
            there = ys[dy]
            ref = stat_y.at[k, there]
            remote(ref, ref, send_sem.at[4, k], y_recv.at[k, there], sibling).wait_recv()
        sums = jnp.sum(stat_y[k], axis=0)
        s_oo, s_goo, s_yo, s_ot, s_got, s_yt = (sums[n : n + 1] for n in range(6))
        inv = 1.0 / jnp.sqrt(s_oo / D + EPSILON)
        stretch = s_ot * inv / D
        centre = (s_goo * inv - s_yo) * inv / D
        tilt = stretch * inv
        centre_dot = (2.0 * inv * s_got - s_yt + tilt * (s_yo - 2.0 * inv * s_goo)) * inv / D
        k1 = inv * inv / tokens
        coef = jnp.concatenate(
            [centre, k1, -2.0 * tilt * k1, -centre_dot * k1, tilt * inv / tokens]
            + [jnp.zeros((123, four), F32)],
            axis=0,
        ).T
        o, t, g = o_s[k], t_s[k], gain[...]
        gy = token_rows(tar, k) * g
        out = (g * g - coef[:, 0:1]) * (t * coef[:, 1:2] + o * coef[:, 2:3])
        out = out + o * coef[:, 3:4] + gy * coef[:, 4:5]
        rows_s[k, core * 4 + x] = out.astype(BF)
        for dx in (2, 1, 3):
            rows_copy(k, core, x, x, at_x(dx)).start()
        rows_copy(k, core, x, 4 + x, sibling).start()

    def share(k):
        for dx in (1, 3, 2):
            there = (x + dx) % 4
            rows_copy(k, core, there, there, sibling).wait_recv()
            rows_copy(k, core, there, 4 + there, sibling).start()

    def backward(k):
        for xx in range(4):
            rows_copy(k, 1 - core, xx, 4 + xx, sibling).wait_recv()
        rhs = rows_s[k].reshape(n_blocks * rows, cols)

        def tile(i, carry):
            at_cols = pl.ds(pl.multiple_of(i * 256, 256), 256)
            lhs = hid[k, :, :, at_cols].reshape(n_blocks * rows, 256)
            prod[at_cols, :] += lax.dot_general(
                lhs, rhs, (((0,), (0,)), ((), ())), preferred_element_type=F32
            )
            return carry

        lax.fori_loop(0, ff // 256, tile, 0)

    ops = dict(forward=forward, pair=pair, stats=stats, stats_y=stats_y, hessian=hessian,
               share=share, backward=backward)

    for k in range(stages):
        loads[k].wait()
    for k in range(min(LEAD, stages)):
        wave(0, k)
    for load in loads[stages:]:
        load.wait()
    vb[...] = vc[...].astype(BF)
    prod[...] = -beta_prev[0] * vp[...]

    def body(i, carry):
        for op, lag in SCHEDULE:
            @pl.when((i >= lag) & (i < stages + lag))
            def _(op=op, lag=lag):
                if isinstance(op, int):
                    wave(op, i - lag)
                else:
                    ops[op](i - lag)

        return carry

    lax.fori_loop(0, stages + max(lag for _, lag in SCHEDULE), body, 0)

    out_copy = pltpu.make_async_copy(prod, update, local_sem.at[stages + 5])
    out_copy.start()
    u, v = prod[...], vc[...]
    v_sq = jnp.sum(v * v)
    along = jnp.sum(u * v)
    own = along / jnp.maximum(v_sq, 1e-30)
    left = u - own * v
    lanes = lax.broadcasted_iota(jnp.int32, (8, 128), 1)
    packed = jnp.zeros((8, 128), F32)
    for n, fact in enumerate((v_sq, along, own, jnp.sum(left * left), jnp.sum(left * v))):
        packed = jnp.where(lanes == n, fact, packed)

    def fact_copy(level, ref, n, to):
        return remote(ref, ref, fact_send.at[level], fact_recv.at[level, n], to)

    fact_z[z] = packed
    for dz in (4, 3, 5, 2, 6, 1, 7):
        fact_copy(0, fact_z.at[z], z, at(dz=dz)).start()
    for dz in range(1, NZ):
        fact_copy(0, fact_z.at[zs[dz]], zs[dz], sibling).wait_recv()
    fact_y[y] = jnp.concatenate([fact_z[n, 0:1, :] for n in range(NZ)], axis=0)
    for dy in (2, 1, 3):
        fact_copy(1, fact_y.at[y], y, at(dy=dy)).start()
    for dy in range(1, NY):
        fact_copy(1, fact_y.at[ys[dy]], ys[dy], sibling).wait_recv()
    fact_t[tp] = fact_y[...].reshape(NY * NZ, 128)
    for d in (4, 5, 3, 2, 6, 7, 1):
        fact_copy(2, fact_t.at[tp], tp, (fs, (tp + d) % NT)).start()
    for d in range(1, NT):
        there = (tp + d) % NT
        fact_copy(2, fact_t.at[there], there, sibling).wait_recv()
    facts = fact_t[...].reshape(NT * NY * NZ, 128)
    scale = 1.0 / (FF * D)
    alpha = jnp.sum(facts[:, 1:2], axis=0, keepdims=True) * scale
    shift = facts[:, 2:3] - alpha
    square = facts[:, 3:4] + shift * (shift * facts[:, 0:1] + 2.0 * facts[:, 4:5])
    beta = jnp.sqrt(jnp.sum(square, axis=0, keepdims=True) * scale)
    facts_out[...] = jnp.where(lanes == 0, alpha, beta)

    def sent(ref, sem):
        pltpu.make_async_copy(ref, ref, sem).wait()

    out_copy.wait()
    for k in range(stages):
        sent(hid.at[k, pl.ds(0, n_blocks - 1)], send_sem.at[0, k])
        sent(sib_out.at[k], send_sem.at[1, k])
        sent(x_out.at[k, pl.ds(0, 3)], send_sem.at[2, k])
        sent(stat_z.at[k, pl.ds(0, 7)], send_sem.at[3, k])
        sent(stat_y.at[k, pl.ds(0, 3)], send_sem.at[4, k])
        sent(rows_s.at[k, pl.ds(0, 7)], send_sem.at[5, k])
    sent(fact_z.at[pl.ds(0, 7)], fact_send.at[0])
    sent(fact_y.at[pl.ds(0, 3)], fact_send.at[1])
    sent(fact_t.at[pl.ds(0, 7)], fact_send.at[2])


def on_device(hidden, residual, target, norm_gain, weight, v_prev, v_cur, beta_prev):
    tokens, ff = hidden.shape
    cols = weight.shape[1]
    rows, blocks = tokens // STAGES, NY * NZ
    _, slots = gather_plan(ff)
    dma = pltpu.SemaphoreType.DMA
    anywhere, vmem = pl.BlockSpec(memory_space=pl.ANY), pl.BlockSpec(memory_space=pltpu.VMEM)
    update, facts = pl.pallas_call(
        kernel,
        out_shape=(jax.ShapeDtypeStruct((ff, cols), F32), jax.ShapeDtypeStruct((8, 128), F32)),
        in_specs=[anywhere] * 3 + [vmem] + [anywhere] * 3 + [pl.BlockSpec(memory_space=pltpu.SMEM)],
        out_specs=(anywhere, vmem),
        scratch_shapes=[
            pltpu.VMEM((STAGES, blocks, rows, ff), BF),
            pltpu.VMEM((ff, cols), BF),
            pltpu.VMEM((ff, cols), BF),
            pltpu.VMEM((ff, cols), F32),
            pltpu.VMEM((ff, cols), F32),
            pltpu.VMEM(residual.shape, BF),
            pltpu.VMEM(target.shape, BF),
            pltpu.VMEM((STAGES, 4, 4 * rows, 2 * cols), BF),
            pltpu.VMEM((STAGES, 4, 4 * rows, 2 * cols), BF),
            pltpu.VMEM((4, 4 * rows, 2 * cols), F32),
            pltpu.VMEM((STAGES, 4, 4 * rows, 2 * cols), BF),
            pltpu.VMEM((STAGES, 4, 4 * rows, 2 * cols), BF),
            pltpu.VMEM((STAGES, 4 * rows, cols), F32),
            pltpu.VMEM((STAGES, 4 * rows, cols), F32),
            pltpu.VMEM((STAGES, NZ, 8, 4 * rows), F32),
            pltpu.VMEM((STAGES, NY, 8, 4 * rows), F32),
            pltpu.VMEM((STAGES, 8, 4 * rows, cols), BF),
            pltpu.VMEM((ff, cols), F32),
            pltpu.VMEM((NZ, 8, 128), F32),
            pltpu.VMEM((NY, NZ, 128), F32),
            pltpu.VMEM((NT, NY * NZ, 128), F32),
            dma((STAGES + 6,)),
            dma((STAGES, slots)),
            dma((STAGES,)),
            dma((STAGES, 4)),
            dma((STAGES, NZ)),
            dma((STAGES, NY)),
            dma((STAGES, 8)),
            dma((3, 8)),
            dma((6, STAGES)),
            dma((3,)),
        ],
        compiler_params=pltpu.CompilerParams(
            collective_id=0, has_side_effects=True, vmem_limit_bytes=60 << 20
        ),
    )(
        hidden, residual, target, norm_gain.reshape(1, cols), weight, v_prev, v_cur,
        beta_prev.reshape(1),
    )
    alpha, beta = facts[0, 0], facts[0, 1]
    return (update - alpha * v_cur) / beta, alpha, beta


def solution(mesh):
    return jax.shard_map(
        on_device,
        mesh=mesh,
        in_specs=(
            P("fsdp", "tp"),
            P("tp", "fsdp"),
            P("tp", "fsdp"),
            P("fsdp"),
            P("tp", "fsdp"),
            P("tp", "fsdp"),
            P("tp", "fsdp"),
            P(),
        ),
        out_specs=(P("tp", "fsdp"), P(), P()),
        check_vma=False,
    )
```

```python
import functools

import jax
import jax.numpy as jnp
from jax import lax
from jax.experimental import pallas as pl
from jax.experimental.pallas import tpu as pltpu
from jax.sharding import PartitionSpec as P

D = 8192
FF = 14336
EPSILON = 1e-05

NY, NZ, NT = 4, 8, 8
GROUPS = ((0, 32, 3), (96, 16, 2))
SPLIT = 1024
SCHEDULE = [
    ("prepare", 1), ("pair", 3), ("stats", 4), ("stats_y", 5), ("hessian", 6), ("share", 7),
    ("backward", 8), (0, -1), (1, 0), (3, 1), (5, 2), (2, 0), (4, 1), (6, 2), ("forward", 2),
]
REFS = 17
BF, F32 = jnp.bfloat16, jnp.float32
MESH = pl.DeviceIdType.MESH


def gather_plan(ff):
    cols = {"a": (0, SPLIT), "b": (SPLIT, ff - SPLIT)}
    size = {"y": NY, "z": NZ}
    order = {"a": ("z", "y"), "b": ("y", "z")}
    slots = {}

    def slot(key):
        return slots.setdefault(key, len(slots))

    def arrivals(part, first, second):
        axes = order[part]
        start, width = cols[part]
        offs = (first, second)
        level = 1 if second else 0
        off, n = offs[level], size[axes[level]]
        if abs(off) * 2 == n:
            half = width // 2
            return [
                ((part, first, second, 0), (start, half), axes[level], -1),
                ((part, first, second, 1), (start + half, half), axes[level], 1),
            ]
        step = -1 if off > 0 else 1
        return [((part, first, second, 0), (start, width), axes[level], step)]

    def offsets(n):
        return [0] + [s * d for d in range(1, n // 2) for s in (1, -1)] + [n // 2]

    waves = [[] for _ in range(NY // 2 + NZ // 2 + 1)]
    for part in ("b", "a"):
        n1, n2 = (size[axis] for axis in order[part])
        for first in offsets(n1):
            for second in offsets(n2):
                recvs = []
                if first or second:
                    recvs = [(slot(key), c) for key, c, _, _ in arrivals(part, first, second)]
                sends = []

                def forward(nf, ns, step):
                    for key, c, axis, s in arrivals(part, nf, ns):
                        if s == step:
                            sends.append((slot(key), c, axis, step))

                for off, n, grow in (
                    (second, n2, lambda o: (first, o)),
                    (first, n1, lambda o: (o, 0)),
                ):
                    if grow(0)[1] == 0 and grow(1)[1] == 0 and second:
                        continue
                    if off >= 0 and off < n // 2:
                        forward(*grow(off + 1), -1)
                    if off <= 0 and -off < n // 2:
                        o = off - 1
                        forward(*grow(n // 2 if -o == n // 2 else o), 1)
                where = (first, second) if order[part][0] == "y" else (second, first)
                waves[abs(first) + abs(second)].append((where, recvs, sends))
    return waves, len(slots)

def kernel(
    hidden, residual, target, gain, weight, v_prev, v_cur, beta_prev,
    update, facts_out,
    hid, w, vb, vc, vp, res, tar, prod, fact_fs, fact_t, v_sq, local_sem, fact_recv, fact_send,
    *of_groups,
):
    n_blocks, local, ff = hid.shape
    cols = w.shape[1]
    tokens = n_blocks * local
    fs, tp = lax.axis_index("fsdp"), lax.axis_index("tp")
    y, z = fs // NZ, fs % NZ
    x, core = tp // 2, tp % 2
    waves, _ = gather_plan(ff)
    ys = [(y + d) % NY for d in range(NY)]
    zs = [(z + d) % NZ for d in range(NZ)]
    z_place = [(q // 4) * 16 + q % 4 for q in zs]

    def place(dy, dz):
        return z_place[dz % NZ] + ys[dy % NY] * 4

    me = place(0, 0)

    def at(dy=0, dz=0):
        return (ys[dy % NY] * NZ + zs[dz % NZ], tp)

    def at_x(dx):
        return (fs, ((x + dx) % 4) * 2 + core)

    sibling = (fs, x * 2 + 1 - core)

    loads = [
        pltpu.make_async_copy(src, dst, local_sem.at[n])
        for n, (src, dst) in enumerate(
            (
                (hidden, hid.at[me]), (weight, w), (v_cur, vc), (residual, res), (target, tar),
                (v_prev, vp),
            )
        )
    ]
    for load in loads:
        load.start()

    barrier = pltpu.get_barrier_semaphore()
    others = [(dy, dz) for dz in (4, 3, 5, 2, 6, 1, 7, 0) for dy in (2, 1, 3, 0) if dy or dz]
    peers = [at(1, 0), at(-1, 0), at(0, 1), at(0, -1)] + [(fs, (tp + d) % NT) for d in range(1, NT)]
    for peer in peers:
        pl.semaphore_signal(barrier, inc=1, device_id=peer, device_id_type=MESH)
    pl.semaphore_wait(barrier, len(peers))

    def remote(src, dst, send, recv, to):
        return pltpu.make_async_remote_copy(
            src_ref=src, dst_ref=dst, send_sem=send, recv_sem=recv,
            device_id=to, device_id_type=MESH,
        )

    def sent(ref, sem):
        pltpu.make_async_copy(ref, ref, sem).wait()

    def steps_of(
        first, rows,
        sib_out, sib_in, half, x_out, x_in, o_s, t_s, stat_z, stat_y, rows_s,
        hid_recv, sib_recv, x_recv, z_recv, y_recv, rows_recv, send_sem,
    ):
        four = 4 * rows
        some = max(1, 256 // four)

        def row(k):
            return pl.multiple_of(first + k * rows, 16)

        def span(k):
            return pl.ds(row(k), rows)

        def hid_copy(k, block, slot, columns, to):
            ref = hid.at[block, span(k), pl.ds(*columns)]
            return remote(ref, ref, send_sem.at[0, k], hid_recv.at[k, slot], to)

        def wave(d, k):
            for where, recvs, sends in waves[d]:
                block = place(*where)
                for slot, columns in recvs:
                    hid_copy(k, block, slot, columns, sibling).wait_recv()
                for slot, columns, axis, step in sends:
                    to = at(dy=step) if axis == "y" else at(dz=step)
                    hid_copy(k, block, slot, columns, to).start()

        def dot_rows(k, c, write):
            def tile(i, carry):
                lhs = hid[pl.ds(c * 16 + i * 4 * some, 4 * some), span(k), :].reshape(some * four, ff)
                for n, rhs in enumerate((w, vb)):
                    out = jnp.dot(lhs, rhs[...], preferred_element_type=F32)
                    write(i, n, out.reshape(some, four, cols))
                return carry

            lax.fori_loop(0, 4 // some, tile, 0)

        def sib_copy(k):
            return remote(sib_out.at[k], sib_in.at[k], send_sem.at[1, k], sib_recv.at[k], sibling)

        def forward(k):
            def to_sibling(i, n, out):
                sib_out[k, pl.ds(i * some, some), :, pl.ds(n * cols, cols)] = out.astype(BF)

            def to_half(i, n, out):
                half[k, pl.ds(i * some, some), :, pl.ds(n * cols, cols)] = out

            dot_rows(k, 1 - core, to_sibling)
            sib_copy(k).start()
            dot_rows(k, core, to_half)

        def x_copy(k, dx, slot):
            there = (x + dx) % 4
            return remote(
                x_out.at[k, there], x_in.at[k, slot], send_sem.at[2, k], x_recv.at[k, slot], at_x(dx)
            )

        def pair(k):
            sib_copy(k).wait_recv()
            for dx in (2, 1, 3):
                there = (x + dx) % 4
                x_out[k, there] = (half[k, there] + sib_in[k, there].astype(F32)).astype(BF)
                x_copy(k, dx, x).start()
            half[k, x] = half[k, x] + sib_in[k, x].astype(F32)

        def token_rows(ref, k):
            return jnp.concatenate(
                [ref[pl.ds(j * local + row(k), rows), :].astype(F32) for j in range(4)], axis=0
            )

        def z_copy(k, dz):
            src = stat_z.at[k, z]
            return remote(src, src, send_sem.at[3, k], z_recv.at[k, z], at(dz=dz))

        def y_copy(k, dy):
            src = stat_y.at[k, y]
            return remote(src, src, send_sem.at[4, k], y_recv.at[k, y], at(dy=dy))

        lane = lax.broadcasted_iota(jnp.int32, (four, 128), 1)

        def stats(k):
            total = half[k, x]
            for dx in (1, 3, 2):
                there = (x + dx) % 4
                x_copy(k, dx, there).wait_recv()
                total = total + x_in[k, there].astype(F32)
            o = total[:, :cols] + token_rows(res, k)
            t = total[:, cols:]
            g = gain[...]
            gy = token_rows(tar, k) * g
            o_s[k] = o
            t_s[k] = t
            g2o = g * g * o
            packed = jnp.zeros((four, 128), F32)
            for n, term in enumerate((o * o, g2o * o, gy * o, o * t, g2o * t, gy * t)):
                packed = jnp.where(lane == n, jnp.sum(term, axis=1, keepdims=True), packed)
            stat_z[k, z] = packed.T[:8]
            for dz in (4, 3, 5, 2, 6, 1, 7):
                z_copy(k, dz).start()

        def stats_y(k):
            for dz in range(1, NZ):
                there = zs[dz]
                ref = stat_z.at[k, there]
                remote(ref, ref, send_sem.at[3, k], z_recv.at[k, there], sibling).wait_recv()
            stat_y[k, y] = jnp.sum(stat_z[k], axis=0)
            for dy in (2, 1, 3):
                y_copy(k, dy).start()

        def rows_copy(k, cc, xx, sem, to):
            ref = rows_s.at[k, cc * 4 + xx]
            return remote(ref, ref, send_sem.at[5, k], rows_recv.at[k, sem], to)

        def hessian(k):
            for dy in range(1, NY):
                there = ys[dy]
                ref = stat_y.at[k, there]
                remote(ref, ref, send_sem.at[4, k], y_recv.at[k, there], sibling).wait_recv()
            sums = jnp.sum(stat_y[k], axis=0)
            s_oo, s_goo, s_yo, s_ot, s_got, s_yt = (sums[n : n + 1] for n in range(6))
            inv = 1.0 / jnp.sqrt(s_oo / D + EPSILON)
            stretch = s_ot * inv / D
            centre = (s_goo * inv - s_yo) * inv / D
            tilt = stretch * inv
            centre_dot = (2.0 * inv * s_got - s_yt + tilt * (s_yo - 2.0 * inv * s_goo)) * inv / D
            k1 = inv * inv / tokens
            coef = jnp.concatenate(
                [centre, k1, -2.0 * tilt * k1, -centre_dot * k1, tilt * inv / tokens]
                + [jnp.zeros((123, four), F32)],
                axis=0,
            ).T
            o, t, g = o_s[k], t_s[k], gain[...]
            gy = token_rows(tar, k) * g
            out = (g * g - coef[:, 0:1]) * (t * coef[:, 1:2] + o * coef[:, 2:3])
            out = out + o * coef[:, 3:4] + gy * coef[:, 4:5]
            rows_s[k, core * 4 + x] = out.astype(BF)
            for dx in (2, 1, 3):
                rows_copy(k, core, x, x, at_x(dx)).start()
            rows_copy(k, core, x, 4 + x, sibling).start()

        def share(k):
            for dx in (1, 3, 2):
                there = (x + dx) % 4
                rows_copy(k, core, there, there, sibling).wait_recv()
                rows_copy(k, core, there, 4 + there, sibling).start()

        def backward(k):
            for xx in range(4):
                rows_copy(k, 1 - core, xx, 4 + xx, sibling).wait_recv()
            rhs = rows_s[k].reshape(n_blocks * rows, cols)

            def tile(i, carry):
                at_cols = pl.ds(pl.multiple_of(i * 256, 256), 256)
                lhs = hid[:, span(k), at_cols].reshape(n_blocks * rows, 256)
                prod[at_cols, :] += lax.dot_general(
                    lhs, rhs, (((0,), (0,)), ((), ())), preferred_element_type=F32
                )
                return carry

            lax.fori_loop(0, ff // 256, tile, 0)

        def drain(k):
            sent(hid.at[pl.ds(0, n_blocks - 1), span(k)], send_sem.at[0, k])
            sent(sib_out.at[k], send_sem.at[1, k])
            sent(x_out.at[k, pl.ds(0, 3)], send_sem.at[2, k])
            sent(stat_z.at[k, pl.ds(0, 7)], send_sem.at[3, k])
            sent(stat_y.at[k, pl.ds(0, 3)], send_sem.at[4, k])
            sent(rows_s.at[k, pl.ds(0, 7)], send_sem.at[5, k])

        return dict(forward=forward, pair=pair, stats=stats, stats_y=stats_y, hessian=hessian,
                    share=share, backward=backward, wave=wave, drain=drain)

    def prepare():
        for load in loads[1:]:
            load.wait()
        vb[...] = vc[...].astype(BF)
        prod[...] = -beta_prev[0] * vp[...]
        v_sq[0] = jnp.sum(vc[...] * vc[...])

    groups, n_stages = [], 0
    for n, (first, rows, stages) in enumerate(GROUPS):
        refs = of_groups[n * REFS : (n + 1) * REFS]
        groups.append((n_stages, stages, steps_of(first, rows, *refs)))
        n_stages += stages

    loads[0].wait()
    groups[0][2]["wave"](0, 0)

    def body(i, carry):
        for op, lag in SCHEDULE:
            if op == "prepare":
                pl.when(i == lag)(prepare)
                continue
            for base, stages, steps in groups:
                k = i - lag - base

                @pl.when((k >= 0) & (k < stages))
                def _(op=op, k=k, steps=steps):
                    if isinstance(op, int):
                        steps["wave"](op, k)
                    else:
                        steps[op](k)

        return carry

    lax.fori_loop(0, n_stages + max(lag for _, lag in SCHEDULE), body, 0)

    out_copy = pltpu.make_async_copy(prod, update, local_sem.at[6])
    out_copy.start()
    u, v = prod[...], vc[...]
    along = jnp.sum(u * v)
    own = along / jnp.maximum(v_sq[0], 1e-30)
    left = u - own * v
    lanes = lax.broadcasted_iota(jnp.int32, (8, 128), 1)

    def pack(values):
        packed = jnp.zeros((8, 128), F32)
        for n, value in enumerate(values):
            packed = jnp.where(lanes == n, value, packed)
        return packed

    def merge(ref):
        facts = ref[:, 0, :]
        square, along, own, left, rest = (facts[:, n : n + 1] for n in range(5))

        def total(part):
            return jnp.sum(part, axis=0, keepdims=True)

        all_square, all_along = total(square), total(along)
        joint = all_along / jnp.maximum(all_square, 1e-30)
        shift = own - joint
        return (
            all_square, all_along, joint,
            total(left + shift * (shift * square + 2.0 * rest)), total(rest + shift * square),
        )

    def fact_copy(level, ref, n, to):
        return remote(ref, ref, fact_send.at[level], fact_recv.at[level, n], to)

    fact_fs[fs] = pack((v_sq[0], along, own, jnp.sum(left * left), jnp.sum(left * v)))
    for dy, dz in others:
        fact_copy(0, fact_fs.at[fs], fs, at(dy, dz)).start()
    for dy, dz in reversed(others):
        there = ys[dy] * NZ + zs[dz]
        fact_copy(0, fact_fs.at[there], there, sibling).wait_recv()
    fact_t[tp] = pack(merge(fact_fs))
    for d in (4, 5, 3, 2, 6, 7, 1):
        fact_copy(1, fact_t.at[tp], tp, (fs, (tp + d) % NT)).start()
    for d in range(1, NT):
        there = (tp + d) % NT
        fact_copy(1, fact_t.at[there], there, sibling).wait_recv()
    scale = 1.0 / (FF * D)
    total, along, joint, left, rest = merge(fact_t)
    alpha = along * scale
    shift = joint - alpha
    square = left + shift * (shift * total + 2.0 * rest)
    beta = jnp.sqrt(square * scale)
    facts_out[...] = jnp.where(lanes == 0, alpha, beta)

    out_copy.wait()
    for _, stages, steps in groups:
        for k in range(stages):
            steps["drain"](k)
    sent(fact_fs.at[pl.ds(0, n_blocks - 1)], fact_send.at[0])
    sent(fact_t.at[pl.ds(0, NT - 1)], fact_send.at[1])


def finish(update, v_cur, facts, out, alpha_out, beta_out):
    alpha, beta = facts[0:1, 0:1], facts[0:1, 1:2]
    out[...] = (update[...] - alpha * v_cur[...]) / beta

    @pl.when(pl.program_id(0) == 0)
    def _():
        alpha_out[0, 0] = facts[0, 0]
        beta_out[0, 0] = facts[0, 1]


def on_device(hidden, residual, target, norm_gain, weight, v_prev, v_cur, beta_prev):
    tokens, ff = hidden.shape
    cols = weight.shape[1]
    blocks = NY * NZ
    _, slots = gather_plan(ff)
    dma = pltpu.SemaphoreType.DMA
    anywhere, vmem = pl.BlockSpec(memory_space=pl.ANY), pl.BlockSpec(memory_space=pltpu.VMEM)
    scratch = [
        pltpu.VMEM((blocks, tokens, ff), BF),
        pltpu.VMEM((ff, cols), BF),
        pltpu.VMEM((ff, cols), BF),
        pltpu.VMEM((ff, cols), F32),
        pltpu.VMEM((ff, cols), F32),
        pltpu.VMEM(residual.shape, BF),
        pltpu.VMEM(target.shape, BF),
        pltpu.VMEM((ff, cols), F32),
        pltpu.VMEM((blocks, 8, 128), F32),
        pltpu.VMEM((NT, 8, 128), F32),
        pltpu.SMEM((1,), F32),
        dma((7,)),
        dma((2, blocks)),
        dma((2,)),
    ]
    for _, rows, stages in GROUPS:
        four = 4 * rows
        scratch += [
            pltpu.VMEM((stages, 4, four, 2 * cols), BF),
            pltpu.VMEM((stages, 4, four, 2 * cols), BF),
            pltpu.VMEM((stages, 4, four, 2 * cols), F32),
            pltpu.VMEM((stages, 4, four, 2 * cols), BF),
            pltpu.VMEM((stages, 4, four, 2 * cols), BF),
            pltpu.VMEM((stages, four, cols), F32),
            pltpu.VMEM((stages, four, cols), F32),
            pltpu.VMEM((stages, NZ, 8, four), F32),
            pltpu.VMEM((stages, NY, 8, four), F32),
            pltpu.VMEM((stages, 8, four, cols), BF),
            dma((stages, slots)),
            dma((stages,)),
            dma((stages, 4)),
            dma((stages, NZ)),
            dma((stages, NY)),
            dma((stages, 8)),
            dma((6, stages)),
        ]
    update, facts = pl.pallas_call(
        kernel,
        out_shape=(jax.ShapeDtypeStruct((ff, cols), F32), jax.ShapeDtypeStruct((8, 128), F32)),
        in_specs=[anywhere] * 3 + [vmem] + [anywhere] * 3 + [pl.BlockSpec(memory_space=pltpu.SMEM)],
        out_specs=(anywhere, vmem),
        scratch_shapes=scratch,
        compiler_params=pltpu.CompilerParams(
            collective_id=0, has_side_effects=True, vmem_limit_bytes=60 << 20
        ),
    )(
        hidden, residual, target, norm_gain.reshape(1, cols), weight, v_prev, v_cur,
        beta_prev.reshape(1),
    )
    strip = pl.BlockSpec((ff // 4, cols), lambda i: (i, 0))
    scalar = pl.BlockSpec(memory_space=pltpu.SMEM)
    one = jax.ShapeDtypeStruct((1, 1), F32)
    v_next, alpha, beta = pl.pallas_call(
        finish,
        out_shape=(jax.ShapeDtypeStruct((ff, cols), F32), one, one),
        grid=(4,),
        in_specs=[strip, strip, pl.BlockSpec((8, 128), lambda i: (0, 0))],
        out_specs=(strip, scalar, scalar),
    )(update, v_cur, facts)
    return v_next, alpha.reshape(()), beta.reshape(())


def solution(mesh):
    return jax.shard_map(
        on_device,
        mesh=mesh,
        in_specs=(
            P("fsdp", "tp"),
            P("tp", "fsdp"),
            P("tp", "fsdp"),
            P("fsdp"),
            P("tp", "fsdp"),
            P("tp", "fsdp"),
            P("tp", "fsdp"),
            P(),
        ),
        out_specs=(P("tp", "fsdp"), P(), P()),
        check_vma=False,
    )
```

```python
import functools

import jax
import jax.numpy as jnp
from jax import lax
from jax.experimental import pallas as pl
from jax.experimental.pallas import tpu as pltpu
from jax.sharding import PartitionSpec as P

D = 8192
FF = 14336
EPSILON = 1e-05

NY, NZ, NT = 4, 8, 8
GROUPS = ((0, 32, 3), (96, 16, 2))
SPLIT = 1024
SCHEDULE = [
    ("pair", 3), ("stats", 4), ("stats_y", 5), ("hessian", 6), ("share", 7), ("backward", 8),
    (0, -1), ("prepare", 0), (1, 0), (3, 1), (5, 2), (2, 0), (4, 1), (6, 2), ("forward", 2),
]
REFS = 17
BF, F32 = jnp.bfloat16, jnp.float32
MESH = pl.DeviceIdType.MESH


def gather_plan(ff):
    cols = {"a": (0, SPLIT), "b": (SPLIT, ff - SPLIT)}
    size = {"y": NY, "z": NZ}
    order = {"a": ("z", "y"), "b": ("y", "z")}
    slots = {}

    def slot(key):
        return slots.setdefault(key, len(slots))

    def arrivals(part, first, second):
        axes = order[part]
        start, width = cols[part]
        offs = (first, second)
        level = 1 if second else 0
        off, n = offs[level], size[axes[level]]
        if abs(off) * 2 == n:
            half = width // 2
            return [
                ((part, first, second, 0), (start, half), axes[level], -1),
                ((part, first, second, 1), (start + half, half), axes[level], 1),
            ]
        step = -1 if off > 0 else 1
        return [((part, first, second, 0), (start, width), axes[level], step)]

    def offsets(n):
        return [0] + [s * d for d in range(1, n // 2) for s in (1, -1)] + [n // 2]

    waves = [[] for _ in range(NY // 2 + NZ // 2 + 1)]
    for part in ("b", "a"):
        n1, n2 = (size[axis] for axis in order[part])
        for first in offsets(n1):
            for second in offsets(n2):
                recvs = []
                if first or second:
                    recvs = [(slot(key), c) for key, c, _, _ in arrivals(part, first, second)]
                sends = []

                def forward(nf, ns, step):
                    for key, c, axis, s in arrivals(part, nf, ns):
                        if s == step:
                            sends.append((slot(key), c, axis, step))

                for off, n, grow in (
                    (second, n2, lambda o: (first, o)),
                    (first, n1, lambda o: (o, 0)),
                ):
                    if grow(0)[1] == 0 and grow(1)[1] == 0 and second:
                        continue
                    if off >= 0 and off < n // 2:
                        forward(*grow(off + 1), -1)
                    if off <= 0 and -off < n // 2:
                        o = off - 1
                        forward(*grow(n // 2 if -o == n // 2 else o), 1)
                where = (first, second) if order[part][0] == "y" else (second, first)
                waves[abs(first) + abs(second)].append((where, recvs, sends))
    return waves, len(slots)

def kernel(
    hidden, residual, target, gain, weight, v_prev, v_cur, beta_prev,
    update, facts_out,
    hid, w, vb, vc, vp, res, tar, prod, fact_fs, fact_t, v_sq, local_sem, fact_recv, fact_send,
    *of_groups,
):
    n_blocks, local, ff = hid.shape
    cols = w.shape[1]
    tokens = n_blocks * local
    fs, tp = lax.axis_index("fsdp"), lax.axis_index("tp")
    y, z = fs // NZ, fs % NZ
    x, core = tp // 2, tp % 2
    waves, _ = gather_plan(ff)
    ys = [(y + d) % NY for d in range(NY)]
    zs = [(z + d) % NZ for d in range(NZ)]
    z_place = [(q // 4) * 16 + q % 4 for q in zs]

    def place(dy, dz):
        return z_place[dz % NZ] + ys[dy % NY] * 4

    me = place(0, 0)

    def at(dy=0, dz=0):
        return (ys[dy % NY] * NZ + zs[dz % NZ], tp)

    def at_x(dx):
        return (fs, ((x + dx) % 4) * 2 + core)

    sibling = (fs, x * 2 + 1 - core)

    loads = [
        pltpu.make_async_copy(src, dst, local_sem.at[n])
        for n, (src, dst) in enumerate(
            (
                (hidden, hid.at[me]), (weight, w), (v_cur, vc), (residual, res), (target, tar),
                (v_prev, vp),
            )
        )
    ]
    for load in loads:
        load.start()

    barrier = pltpu.get_barrier_semaphore()
    others = [(dy, dz) for dz in (4, 3, 5, 2, 6, 1, 7, 0) for dy in (2, 1, 3, 0) if dy or dz]
    peers = [at(1, 0), at(-1, 0), at(0, 1), at(0, -1)] + [(fs, (tp + d) % NT) for d in range(1, NT)]
    for peer in peers:
        pl.semaphore_signal(barrier, inc=1, device_id=peer, device_id_type=MESH)
    pl.semaphore_wait(barrier, len(peers))

    def remote(src, dst, send, recv, to):
        return pltpu.make_async_remote_copy(
            src_ref=src, dst_ref=dst, send_sem=send, recv_sem=recv,
            device_id=to, device_id_type=MESH,
        )

    def sent(ref, sem):
        pltpu.make_async_copy(ref, ref, sem).wait()

    def steps_of(
        first, rows,
        sib_out, sib_in, half, x_out, x_in, o_s, t_s, stat_z, stat_y, rows_s,
        hid_recv, sib_recv, x_recv, z_recv, y_recv, rows_recv, send_sem,
    ):
        four = 4 * rows
        some = max(1, 256 // four)

        def row(k):
            return pl.multiple_of(first + k * rows, 16)

        def span(k):
            return pl.ds(row(k), rows)

        def hid_copy(k, block, slot, columns, to):
            ref = hid.at[block, span(k), pl.ds(*columns)]
            return remote(ref, ref, send_sem.at[0, k], hid_recv.at[k, slot], to)

        def wave(d, k):
            for where, recvs, sends in waves[d]:
                block = place(*where)
                for slot, columns in recvs:
                    hid_copy(k, block, slot, columns, sibling).wait_recv()
                for slot, columns, axis, step in sends:
                    to = at(dy=step) if axis == "y" else at(dz=step)
                    hid_copy(k, block, slot, columns, to).start()

        def dot_rows(k, c, write):
            def tile(i, carry):
                lhs = hid[pl.ds(c * 16 + i * 4 * some, 4 * some), span(k), :].reshape(some * four, ff)
                for n, rhs in enumerate((w, vb)):
                    out = jnp.dot(lhs, rhs[...], preferred_element_type=F32)
                    write(i, n, out.reshape(some, four, cols))
                return carry

            lax.fori_loop(0, 4 // some, tile, 0)

        def sib_copy(k):
            return remote(sib_out.at[k], sib_in.at[k], send_sem.at[1, k], sib_recv.at[k], sibling)

        def forward(k):
            def to_sibling(i, n, out):
                sib_out[k, pl.ds(i * some, some), :, pl.ds(n * cols, cols)] = out.astype(BF)

            def to_half(i, n, out):
                half[k, pl.ds(i * some, some), :, pl.ds(n * cols, cols)] = out

            dot_rows(k, 1 - core, to_sibling)
            sib_copy(k).start()
            dot_rows(k, core, to_half)

        def x_copy(k, dx, slot):
            there = (x + dx) % 4
            return remote(
                x_out.at[k, there], x_in.at[k, slot], send_sem.at[2, k], x_recv.at[k, slot], at_x(dx)
            )

        def pair(k):
            sib_copy(k).wait_recv()
            for dx in (2, 1, 3):
                there = (x + dx) % 4
                x_out[k, there] = (half[k, there] + sib_in[k, there].astype(F32)).astype(BF)
                x_copy(k, dx, x).start()
            half[k, x] = half[k, x] + sib_in[k, x].astype(F32)

        def token_rows(ref, k):
            return jnp.concatenate(
                [ref[pl.ds(j * local + row(k), rows), :].astype(F32) for j in range(4)], axis=0
            )

        def z_copy(k, dz):
            src = stat_z.at[k, z]
            return remote(src, src, send_sem.at[3, k], z_recv.at[k, z], at(dz=dz))

        def y_copy(k, dy):
            src = stat_y.at[k, y]
            return remote(src, src, send_sem.at[4, k], y_recv.at[k, y], at(dy=dy))

        lane = lax.broadcasted_iota(jnp.int32, (four, 128), 1)

        def stats(k):
            total = half[k, x]
            for dx in (1, 3, 2):
                there = (x + dx) % 4
                x_copy(k, dx, there).wait_recv()
                total = total + x_in[k, there].astype(F32)
            o = total[:, :cols] + token_rows(res, k)
            t = total[:, cols:]
            g = gain[...]
            gy = token_rows(tar, k) * g
            o_s[k] = o
            t_s[k] = t
            g2o = g * g * o
            packed = jnp.zeros((four, 128), F32)
            for n, term in enumerate((o * o, g2o * o, gy * o, o * t, g2o * t, gy * t)):
                packed = jnp.where(lane == n, jnp.sum(term, axis=1, keepdims=True), packed)
            stat_z[k, z] = packed.T[:8]
            for dz in (4, 3, 5, 2, 6, 1, 7):
                z_copy(k, dz).start()

        def stats_y(k):
            for dz in range(1, NZ):
                there = zs[dz]
                ref = stat_z.at[k, there]
                remote(ref, ref, send_sem.at[3, k], z_recv.at[k, there], sibling).wait_recv()
            stat_y[k, y] = jnp.sum(stat_z[k], axis=0)
            for dy in (2, 1, 3):
                y_copy(k, dy).start()

        def rows_copy(k, cc, xx, sem, to):
            ref = rows_s.at[k, cc * 4 + xx]
            return remote(ref, ref, send_sem.at[5, k], rows_recv.at[k, sem], to)

        def hessian(k):
            for dy in range(1, NY):
                there = ys[dy]
                ref = stat_y.at[k, there]
                remote(ref, ref, send_sem.at[4, k], y_recv.at[k, there], sibling).wait_recv()
            sums = jnp.sum(stat_y[k], axis=0)
            s_oo, s_goo, s_yo, s_ot, s_got, s_yt = (sums[n : n + 1] for n in range(6))
            inv = 1.0 / jnp.sqrt(s_oo / D + EPSILON)
            stretch = s_ot * inv / D
            centre = (s_goo * inv - s_yo) * inv / D
            tilt = stretch * inv
            centre_dot = (2.0 * inv * s_got - s_yt + tilt * (s_yo - 2.0 * inv * s_goo)) * inv / D
            k1 = inv * inv / tokens
            coef = jnp.concatenate(
                [centre, k1, -2.0 * tilt * k1, -centre_dot * k1, tilt * inv / tokens]
                + [jnp.zeros((123, four), F32)],
                axis=0,
            ).T
            o, t, g = o_s[k], t_s[k], gain[...]
            gy = token_rows(tar, k) * g
            out = (g * g - coef[:, 0:1]) * (t * coef[:, 1:2] + o * coef[:, 2:3])
            out = out + o * coef[:, 3:4] + gy * coef[:, 4:5]
            rows_s[k, core * 4 + x] = out.astype(BF)
            for dx in (2, 1, 3):
                rows_copy(k, core, x, x, at_x(dx)).start()
            rows_copy(k, core, x, 4 + x, sibling).start()

        def share(k):
            for dx in (1, 3, 2):
                there = (x + dx) % 4
                rows_copy(k, core, there, there, sibling).wait_recv()
                rows_copy(k, core, there, 4 + there, sibling).start()

        def backward(k):
            for xx in range(4):
                rows_copy(k, 1 - core, xx, 4 + xx, sibling).wait_recv()
            rhs = rows_s[k].reshape(n_blocks * rows, cols)

            def tile(i, carry):
                at_cols = pl.ds(pl.multiple_of(i * 256, 256), 256)
                lhs = hid[:, span(k), at_cols].reshape(n_blocks * rows, 256)
                prod[at_cols, :] += lax.dot_general(
                    lhs, rhs, (((0,), (0,)), ((), ())), preferred_element_type=F32
                )
                return carry

            lax.fori_loop(0, ff // 256, tile, 0)

        def drain(k):
            sent(hid.at[pl.ds(0, n_blocks - 1), span(k)], send_sem.at[0, k])
            sent(sib_out.at[k], send_sem.at[1, k])
            sent(x_out.at[k, pl.ds(0, 3)], send_sem.at[2, k])
            sent(stat_z.at[k, pl.ds(0, 7)], send_sem.at[3, k])
            sent(stat_y.at[k, pl.ds(0, 3)], send_sem.at[4, k])
            sent(rows_s.at[k, pl.ds(0, 7)], send_sem.at[5, k])

        return dict(forward=forward, pair=pair, stats=stats, stats_y=stats_y, hessian=hessian,
                    share=share, backward=backward, wave=wave, drain=drain)

    def prepare():
        for load in loads[1:]:
            load.wait()
        vb[...] = vc[...].astype(BF)
        prod[...] = -beta_prev[0] * vp[...]
        v_sq[0] = jnp.sum(vc[...] * vc[...])

    groups, n_stages = [], 0
    for n, (first, rows, stages) in enumerate(GROUPS):
        refs = of_groups[n * REFS : (n + 1) * REFS]
        groups.append((n_stages, stages, steps_of(first, rows, *refs)))
        n_stages += stages

    loads[0].wait()
    groups[0][2]["wave"](0, 0)

    def body(i, carry):
        for op, lag in SCHEDULE:
            if op == "prepare":
                pl.when(i == lag)(prepare)
                continue
            for base, stages, steps in groups:
                k = i - lag - base

                @pl.when((k >= 0) & (k < stages))
                def _(op=op, k=k, steps=steps):
                    if isinstance(op, int):
                        steps["wave"](op, k)
                    else:
                        steps[op](k)

        return carry

    lax.fori_loop(0, n_stages + max(lag for _, lag in SCHEDULE), body, 0)

    out_copy = pltpu.make_async_copy(prod, update, local_sem.at[6])
    out_copy.start()
    u, v = prod[...], vc[...]
    along = jnp.sum(u * v)
    own = along / jnp.maximum(v_sq[0], 1e-30)
    left = u - own * v
    lanes = lax.broadcasted_iota(jnp.int32, (8, 128), 1)

    def pack(values):
        packed = jnp.zeros((8, 128), F32)
        for n, value in enumerate(values):
            packed = jnp.where(lanes == n, value, packed)
        return packed

    def merge(ref):
        facts = ref[:, 0, :]
        square, along, own, left, rest = (facts[:, n : n + 1] for n in range(5))

        def total(part):
            return jnp.sum(part, axis=0, keepdims=True)

        all_square, all_along = total(square), total(along)
        joint = all_along / jnp.maximum(all_square, 1e-30)
        shift = own - joint
        return (
            all_square, all_along, joint,
            total(left + shift * (shift * square + 2.0 * rest)), total(rest + shift * square),
        )

    def fact_copy(level, ref, n, to):
        return remote(ref, ref, fact_send.at[level], fact_recv.at[level, n], to)

    fact_fs[fs] = pack((v_sq[0], along, own, jnp.sum(left * left), jnp.sum(left * v)))
    for dy, dz in others:
        fact_copy(0, fact_fs.at[fs], fs, at(dy, dz)).start()
    for dy, dz in reversed(others):
        there = ys[dy] * NZ + zs[dz]
        fact_copy(0, fact_fs.at[there], there, sibling).wait_recv()
    fact_t[tp] = pack(merge(fact_fs))
    for d in (4, 5, 3, 2, 6, 7, 1):
        fact_copy(1, fact_t.at[tp], tp, (fs, (tp + d) % NT)).start()
    for d in range(1, NT):
        there = (tp + d) % NT
        fact_copy(1, fact_t.at[there], there, sibling).wait_recv()
    scale = 1.0 / (FF * D)
    total, along, joint, left, rest = merge(fact_t)
    alpha = along * scale
    shift = joint - alpha
    square = left + shift * (shift * total + 2.0 * rest)
    beta = jnp.sqrt(square * scale)
    facts_out[...] = jnp.where(lanes == 0, alpha, beta)

    out_copy.wait()
    for _, stages, steps in groups:
        for k in range(stages):
            steps["drain"](k)
    sent(fact_fs.at[pl.ds(0, n_blocks - 1)], fact_send.at[0])
    sent(fact_t.at[pl.ds(0, NT - 1)], fact_send.at[1])


def finish(update, v_cur, facts, out, alpha_out, beta_out):
    alpha, beta = facts[0:1, 0:1], facts[0:1, 1:2]
    out[...] = (update[...] - alpha * v_cur[...]) / beta

    @pl.when(pl.program_id(0) == 0)
    def _():
        alpha_out[0, 0] = facts[0, 0]
        beta_out[0, 0] = facts[0, 1]


def on_device(hidden, residual, target, norm_gain, weight, v_prev, v_cur, beta_prev):
    tokens, ff = hidden.shape
    cols = weight.shape[1]
    blocks = NY * NZ
    _, slots = gather_plan(ff)
    dma = pltpu.SemaphoreType.DMA
    anywhere, vmem = pl.BlockSpec(memory_space=pl.ANY), pl.BlockSpec(memory_space=pltpu.VMEM)
    scratch = [
        pltpu.VMEM((blocks, tokens, ff), BF),
        pltpu.VMEM((ff, cols), BF),
        pltpu.VMEM((ff, cols), BF),
        pltpu.VMEM((ff, cols), F32),
        pltpu.VMEM((ff, cols), F32),
        pltpu.VMEM(residual.shape, BF),
        pltpu.VMEM(target.shape, BF),
        pltpu.VMEM((ff, cols), F32),
        pltpu.VMEM((blocks, 8, 128), F32),
        pltpu.VMEM((NT, 8, 128), F32),
        pltpu.SMEM((1,), F32),
        dma((7,)),
        dma((2, blocks)),
        dma((2,)),
    ]
    for _, rows, stages in GROUPS:
        four = 4 * rows
        scratch += [
            pltpu.VMEM((stages, 4, four, 2 * cols), BF),
            pltpu.VMEM((stages, 4, four, 2 * cols), BF),
            pltpu.VMEM((stages, 4, four, 2 * cols), F32),
            pltpu.VMEM((stages, 4, four, 2 * cols), BF),
            pltpu.VMEM((stages, 4, four, 2 * cols), BF),
            pltpu.VMEM((stages, four, cols), F32),
            pltpu.VMEM((stages, four, cols), F32),
            pltpu.VMEM((stages, NZ, 8, four), F32),
            pltpu.VMEM((stages, NY, 8, four), F32),
            pltpu.VMEM((stages, 8, four, cols), BF),
            dma((stages, slots)),
            dma((stages,)),
            dma((stages, 4)),
            dma((stages, NZ)),
            dma((stages, NY)),
            dma((stages, 8)),
            dma((6, stages)),
        ]
    update, facts = pl.pallas_call(
        kernel,
        out_shape=(jax.ShapeDtypeStruct((ff, cols), F32), jax.ShapeDtypeStruct((8, 128), F32)),
        in_specs=[anywhere] * 3 + [vmem] + [anywhere] * 3 + [pl.BlockSpec(memory_space=pltpu.SMEM)],
        out_specs=(anywhere, vmem),
        scratch_shapes=scratch,
        compiler_params=pltpu.CompilerParams(
            collective_id=0, has_side_effects=True, vmem_limit_bytes=60 << 20
        ),
    )(
        hidden, residual, target, norm_gain.reshape(1, cols), weight, v_prev, v_cur,
        beta_prev.reshape(1),
    )
    strip = pl.BlockSpec((ff // 4, cols), lambda i: (i, 0))
    scalar = pl.BlockSpec(memory_space=pltpu.SMEM)
    one = jax.ShapeDtypeStruct((1, 1), F32)
    v_next, alpha, beta = pl.pallas_call(
        finish,
        out_shape=(jax.ShapeDtypeStruct((ff, cols), F32), one, one),
        grid=(4,),
        in_specs=[strip, strip, pl.BlockSpec((8, 128), lambda i: (0, 0))],
        out_specs=(strip, scalar, scalar),
    )(update, v_cur, facts)
    return v_next, alpha.reshape(()), beta.reshape(())


def solution(mesh):
    return jax.shard_map(
        on_device,
        mesh=mesh,
        in_specs=(
            P("fsdp", "tp"),
            P("tp", "fsdp"),
            P("tp", "fsdp"),
            P("fsdp"),
            P("tp", "fsdp"),
            P("tp", "fsdp"),
            P("tp", "fsdp"),
            P(),
        ),
        out_specs=(P("tp", "fsdp"), P(), P()),
        check_vma=False,
    )
```
